32 devices in a mesh: region: 4 (over y, core), group: 8 (over z, x).
Axes of the slice: x: 2, y: 2, z: 4, core: 2. Of those that a mesh axis runs over, the one named last changes fastest.
Arguments:
- phi: bfloat16 [1024, 12288], P('group', 'region'), may hold values from -6 to 6
- hphi: bfloat16 [1024, 12288], P('group', 'region'), may hold values from -6 to 6
- extents: int32 [1024, 2], P('group'), may hold values from 0 to 12288, as said below
- columns: int32 [8, 3], replicated, may hold values from 0 to 7, as said below
- kernel: bfloat16 [8, 3, 128, 128], replicated, may hold values from -0.3125 to 0.3125
Outputs:
- gradient: bfloat16 [1024, 12288], P('group', 'region')
- lagrange: float32 [8, 3, 128, 128], P('group')
The draws below stay inside these ranges and needn't reach their ends.
Inputs may be any that keep to these rules, and one draw needn't show every extreme that they name: extents[f, 0] < extents[f, 1]; each region starts at or before point 12288 - 3 * 3072 and spans 9216 to 18432 points before it is cut at the grid's end. Each block row lists 3 distinct block columns, the first being the row itself.
All inputs are finite; a program needn't handle non-finite values.
Results may differ from the reference program's by a relative error of at most 0.005.
Values may be sent and summed in bfloat16 or wider, within the bound.
A program may use at most 128 MiB of HBM per device.

```python
import jax
import jax.numpy as jnp
from jax import lax

BLK = 128
NBR = 3
PD = 384
NB = 8
NF = 1024
REGPTS = 3072
NPTS = 12288


def draw_extents(key, part):
    first, second = jax.random.split(jax.random.fold_in(key, 11))
    low = jax.random.randint(first, (NF,), 0, NPTS - 3 * REGPTS + 1)
    length = jax.random.randint(second, (NF,), 3 * REGPTS, 6 * REGPTS + 1)
    high = jnp.minimum(low + length, NPTS)
    low = low.at[0].set(0)
    high = high.at[NF - 1].set(NPTS)
    return jnp.stack([low, high], axis=1).astype(jnp.int32)


def draw_columns(key, part):
    keys = jax.random.split(jax.random.fold_in(key, 23), NB)

    def one_row(row_key):
        return jax.random.permutation(row_key, NB - 1)[:NBR - 1] + 1
    offsets = jax.vmap(one_row)(keys)
    offsets = jnp.concatenate([jnp.zeros((NB, 1), jnp.int32), offsets.astype(jnp.int32)], axis=1)
    return ((jnp.arange(NB, dtype=jnp.int32)[:, None] + offsets) % NB).astype(jnp.int32)


def block_levels(stream_key, dims, cuts, low, largest):
    factor_of = 1.0
    for axis_at, shards_of in cuts:
        heights = jax.random.uniform(jax.random.fold_in(jax.random.fold_in(stream_key, 6), axis_at), (shards_of,), jnp.float32, low / len(cuts), largest / len(cuts))
        factor_of = factor_of * jnp.repeat(jnp.exp(heights), dims[axis_at] // shards_of).reshape((-1,) + (1,) * (len(dims) - 1 - axis_at))
    return factor_of


def centred(own_key, dims, spread, bound, cuts=(), kind=jnp.bfloat16):
    level = block_levels(own_key, dims, cuts, -0.22, 0.18) if cuts else 1.0
    result = jax.random.normal(own_key, dims, jnp.float32) * spread * level
    return jnp.minimum(jnp.maximum(result, -bound), bound).astype(kind)


def setup_inputs(seed: int = 0) -> dict:
    seeds = jax.random.split(jax.random.key(seed), 6)
    return {
        "phi": centred(seeds[0], (NF, NPTS), 1.0, 6.0, ((0, 8), (1, 4))),
        "hphi": centred(seeds[1], (NF, NPTS), 1.0, 6.0, ((0, 8), (1, 4))),
        "extents": draw_extents(jax.random.fold_in(seeds[5], 71), 0),
        "columns": draw_columns(jax.random.fold_in(seeds[5], 71), 0),
        "kernel": centred(seeds[4], (NB, NBR, BLK, BLK), (BLK * NBR) ** -0.5, 0.3125),
    }


def reference(phi, hphi, extents, columns, kernel):
    slabs = NPTS // PD
    low = extents[:, 0:1]
    high = extents[:, 1:2]
    zero = jnp.zeros((), jnp.bfloat16)

    def pieces(index):
        start = index * PD
        point = start + lax.broadcasted_iota(jnp.int32, (NF, PD), 1)
        inside = (point >= low) & (point < high)
        phi_loc = jnp.where(inside, lax.dynamic_slice_in_dim(phi, start, PD, 1), zero)
        hphi_loc = jnp.where(inside, lax.dynamic_slice_in_dim(hphi, start, PD, 1), zero)
        return inside, phi_loc, hphi_loc

    def accumulate(total, index):
        inside, phi_loc, hphi_loc = pieces(index)
        shifted = (hphi_loc.astype(jnp.float32) + 0.5 * phi_loc.astype(jnp.float32)).astype(jnp.bfloat16)
        left = phi_loc.reshape(NB, BLK, PD).astype(jnp.float32)
        right = shifted.reshape(NB, BLK, PD)[columns].astype(jnp.float32)
        return total + jnp.einsum("aip,ajkp->ajik", left, right), None

    steps = jnp.arange(slabs, dtype=jnp.int32)
    total, unused = lax.scan(accumulate, jnp.zeros((NB, NBR, BLK, BLK), jnp.float32), steps)
    lagrange = total * (1.0 / REGPTS)
    lagrange = lagrange.at[:, 0].add(-0.5 * jnp.eye(BLK, dtype=jnp.float32))
    lagrange_low = lagrange.astype(jnp.bfloat16).astype(jnp.float32)
    kernel_wide = kernel.astype(jnp.float32)

    def descend(carry, index):
        inside, phi_loc, hphi_loc = pieces(index)
        hx = hphi_loc.reshape(NB, BLK, PD)[columns].astype(jnp.float32)
        px = phi_loc.reshape(NB, BLK, PD)[columns].astype(jnp.float32)
        raw = jnp.einsum("ajik,ajkp->aip", kernel_wide, hx) - jnp.einsum("ajik,ajkp->aip", lagrange_low, px)
        raw = raw.reshape(NF, PD).astype(jnp.bfloat16)
        return carry, jnp.where(inside, raw, zero)

    unused, parts = lax.scan(descend, jnp.zeros((), jnp.float32), steps)
    gradient = jnp.transpose(parts, (1, 0, 2)).reshape(NF, NPTS)
    return gradient, lagrange
```

```python
import functools

import jax
import jax.numpy as jnp
from jax import lax
from jax.experimental import pallas as pl
from jax.experimental.pallas import tpu as pltpu
from jax.sharding import PartitionSpec as P

F32 = jnp.float32
BF16 = jnp.bfloat16


def body(n, nreg, phi, hphi, ext, col, ker, grad, lag,
         src, grid, shift, part, cbuf, ybuf, red, gbuf, low, fbuf, kh, ret,
         as_, ar, cs, cr, ys, yr, gs, gr, ls, lr, fs, fr, lys, lyr, lcs, lcr, bs, br):
    rows, width = phi.shape
    depth = width // n
    nbr = col.shape[1]
    pairs = nreg // 2
    slab = rows // nreg
    me = lax.axis_index("group")
    r = lax.axis_index("region")
    q = r // 2
    c = r % 2
    partner = 2 * q + 1 - c

    def to_group(a, b, s1, s2, k):
        return pltpu.make_async_remote_copy(
            src_ref=a, dst_ref=b, send_sem=s1, recv_sem=s2,
            device_id={"group": k}, device_id_type=pl.DeviceIdType.MESH)

    def to_region(a, b, s1, s2, k):
        return pltpu.make_async_remote_copy(
            src_ref=a, dst_ref=b, send_sem=s1, recv_sem=s2,
            device_id={"region": k}, device_id_type=pl.DeviceIdType.MESH)

    def each(lo, hi, f):
        def step(s, carry):
            f(s)
            return carry
        lax.fori_loop(lo, hi, step, 0)

    up = lambda s: lax.rem(me + s, n)
    down = lambda s: lax.rem(me + n - s, n)
    rup = lambda t: lax.rem(r + t, nreg)
    qup = lambda t: lax.rem(q + t, pairs)

    barrier = pltpu.get_barrier_semaphore()
    each(1, n, lambda s: pl.semaphore_signal(
        barrier, inc=1, device_id={"group": up(s)}, device_id_type=pl.DeviceIdType.MESH))
    each(1, nreg, lambda t: pl.semaphore_signal(
        barrier, inc=1, device_id={"region": rup(t)}, device_id_type=pl.DeviceIdType.MESH))

    first = ext[:, 0:1]
    last = ext[:, 1:2]

    def inside(k):
        point = r * width + k * depth + lax.broadcasted_iota(jnp.int32, (rows, depth), 1)
        return (point >= first) & (point < last)

    def cut(k):
        return pl.ds(pl.multiple_of(k * depth, 128), depth)

    def masked(ref, k):
        return jnp.where(inside(k), ref[:, cut(k)].astype(F32), 0.0).astype(BF16)

    def shifted(k):
        shift[k] = (grid[k, 1].astype(F32) + 0.5 * grid[k, 0].astype(F32)).astype(BF16)

    grid[me, 0] = masked(phi, me)
    grid[me, 1] = masked(hphi, me)
    shifted(me)
    pl.semaphore_wait(barrier, n - 1 + nreg - 1)

    def out_copy(k):
        return to_group(src.at[k], grid.at[me], as_.at[k], ar.at[me], k)

    def send_out(s):
        k = up(s)
        src[k, 0] = masked(phi, k)
        src[k, 1] = masked(hphi, k)
        out_copy(k).start()
    each(1, n, send_out)

    def take_in(s):
        k = down(s)
        to_group(src.at[k], grid.at[k], as_.at[k], ar.at[k], k).wait_recv()
        shifted(k)
    each(1, n, take_in)

    def core_copy(p, a):
        return to_region(part.at[1 - c, p, a], cbuf.at[p, a], cs.at[p, a], cr.at[p, a], partner)

    def partial(s):
        a = up(s)
        left = grid[a, 0]
        for j in range(nbr):
            res = lax.dot_general(left, shift[col[a, j]], (((1,), (1,)), ((), ())),
                                  preferred_element_type=F32)
            for i in range(nreg):
                part[i % 2, i // 2, a, j] = res[i * slab:(i + 1) * slab]
        each(1, pairs + 1, lambda t: core_copy(qup(t), a).start())
    each(1, n + 1, partial)

    def y_copy(p, a):
        return to_region(part.at[c, p, a], ybuf.at[q, a], ys.at[p, a], yr.at[q, a], 2 * p + c)

    def y_wait(p, a):
        to_region(part.at[c, p, a], ybuf.at[p, a], ys.at[p, a], yr.at[p, a], 2 * p + c).wait_recv()

    def forward(s):
        a = up(s)

        def one(t):
            p = qup(t)
            core_copy(p, a).wait_recv()
            part[c, p, a] = part[c, p, a] + cbuf[p, a]
            y_copy(p, a).start()
        each(1, pairs, one)
    each(1, n + 1, forward)

    def red_copy(k):
        return to_group(red.at[k], gbuf.at[me], gs.at[k], gr.at[me], k)

    def reduce_one(a):
        total = jnp.zeros((rows, depth), F32)
        for j in range(nbr):
            total = total + jnp.dot(ker[a, j], grid[col[a, j], 1], preferred_element_type=F32)
        kh[a] = total
        core_copy(q, a).wait_recv()
        red[a] = part[c, q, a] + cbuf[q, a]

        def one(t):
            p = qup(t)
            y_wait(p, a)
            red[a] = red[a] + ybuf[p, a]
        each(1, pairs, one)

    def reduce_send(s):
        a = up(s)
        reduce_one(a)
        red_copy(a).start()
    each(1, n, reduce_send)
    reduce_one(me)

    def gather_sum(s):
        k = down(s)
        to_group(red.at[k], gbuf.at[k], gs.at[k], gr.at[k], k).wait_recv()
        red[me] = red[me] + gbuf[k]
    each(1, n, gather_sum)

    slot = lax.broadcasted_iota(jnp.int32, (nbr, slab, rows), 0)
    row = r * slab + lax.broadcasted_iota(jnp.int32, (nbr, slab, rows), 1)
    column = lax.broadcasted_iota(jnp.int32, (nbr, slab, rows), 2)
    eye = jnp.where((slot == 0) & (row == column), 0.5, 0.0)
    full = red[me] * (1.0 / width) - eye
    fbuf[r] = full
    low[c, q, me] = full.astype(BF16)

    def low_copy(k):
        return to_group(low.at[c, q, me], low.at[c, q, me], ls.at[k], lr.at[me], k)

    def low_wait(k):
        to_group(low.at[c, q, k], low.at[c, q, k], ls.at[k], lr.at[k], k).wait_recv()

    def ly_copy(p, k):
        return to_region(low.at[c, q, k], low.at[c, q, k], lys.at[p, k], lyr.at[q, k], 2 * p + c)

    def ly_wait(p, k):
        to_region(low.at[c, p, k], low.at[c, p, k], lys.at[p, k], lyr.at[p, k],
                  2 * p + c).wait_recv()

    def lc_copy(p, k):
        return to_region(low.at[c, p, k], low.at[c, p, k], lcs.at[p, k], lcr.at[p, k], partner)

    def lc_wait(p, k):
        to_region(low.at[1 - c, p, k], low.at[1 - c, p, k], lcs.at[p, k], lcr.at[p, k],
                  partner).wait_recv()

    def full_copy(i):
        return to_region(fbuf.at[r], fbuf.at[r], fs.at[i], fr.at[r], i)

    each(1, n, lambda s: low_copy(up(s)).start())

    def spread(s):
        k = down(s)
        low_wait(k)
        each(1, pairs, lambda t: ly_copy(qup(t), k).start())
        lc_copy(q, k).start()
    each(1, n, spread)
    each(1, pairs, lambda t: ly_copy(qup(t), me).start())
    lc_copy(q, me).start()
    each(1, nreg, lambda t: full_copy(rup(t)).start())

    def relay(s):
        k = down(s)

        def one(t):
            p = qup(t)
            ly_wait(p, k)
            lc_copy(p, k).start()
        each(1, pairs, one)
    each(1, n + 1, relay)

    def back_copy(a):
        return to_group(shift.at[a], ret.at[me], bs.at[a], br.at[me], a)

    def descend(a):
        each(0, pairs, lambda p: lc_wait(p, a))
        total = kh[a]
        for j in range(nbr):
            block = jnp.concatenate([low[i % 2, i // 2, a, j] for i in range(nreg)], axis=0)
            total = total - jnp.dot(block, grid[col[a, j], 0], preferred_element_type=F32)
        return total.astype(BF16)

    def send_back(s):
        a = down(s)
        shift[a] = descend(a)
        back_copy(a).start()
    each(1, n, send_back)

    def store(k, value):
        grad[:, cut(k)] = jnp.where(inside(k), value.astype(F32), 0.0).astype(BF16)

    store(me, descend(me))

    def finish(s):
        k = up(s)
        to_group(shift.at[k], ret.at[k], bs.at[k], br.at[k], k).wait_recv()
        store(k, ret[k])
    each(1, n, finish)

    def full_wait(t):
        i = rup(t)
        to_region(fbuf.at[i], fbuf.at[i], fs.at[i], fr.at[i], i).wait_recv()
    each(1, nreg, full_wait)
    for i in range(nreg):
        for j in range(nbr):
            lag[0, j, i * slab:(i + 1) * slab, :] = fbuf[i, j]

    def drain(s):
        k = up(s)
        out_copy(k).wait_send()
        red_copy(k).wait_send()
        low_copy(k).wait_send()
        back_copy(k).wait_send()
    each(1, n, drain)
    each(1, nreg, lambda t: full_copy(rup(t)).wait_send())

    def drain_region(a):
        def own(p):
            core_copy(p, a).wait_send()
            lc_copy(p, a).wait_send()

        def other(t):
            y_copy(qup(t), a).wait_send()
            ly_copy(qup(t), a).wait_send()
        each(0, pairs, own)
        each(1, pairs, other)
    each(0, n, drain_region)


def shards(phi, hphi, extents, columns, kernel):
    rows, width = phi.shape
    n = lax.axis_size("group")
    nreg = lax.axis_size("region")
    nbr = columns.shape[1]
    depth = width // n
    pairs = nreg // 2
    slab = rows // nreg
    dma = pltpu.SemaphoreType.DMA
    vmem = pl.BlockSpec(memory_space=pltpu.VMEM)
    smem = pl.BlockSpec(memory_space=pltpu.SMEM)
    return pl.pallas_call(
        functools.partial(body, n, nreg),
        out_shape=(jax.ShapeDtypeStruct((rows, width), BF16),
                   jax.ShapeDtypeStruct((1, nbr, rows, rows), F32)),
        in_specs=[vmem, vmem, vmem, smem, vmem],
        out_specs=(vmem, vmem),
        scratch_shapes=[
            pltpu.VMEM((n, 2, rows, depth), BF16),
            pltpu.VMEM((n, 2, rows, depth), BF16),
            pltpu.VMEM((n, rows, depth), BF16),
            pltpu.VMEM((2, pairs, n, nbr, slab, rows), F32),
            pltpu.VMEM((pairs, n, nbr, slab, rows), F32),
            pltpu.VMEM((pairs, n, nbr, slab, rows), F32),
            pltpu.VMEM((n, nbr, slab, rows), F32),
            pltpu.VMEM((n, nbr, slab, rows), F32),
            pltpu.VMEM((2, pairs, n, nbr, slab, rows), BF16),
            pltpu.VMEM((nreg, nbr, slab, rows), F32),
            pltpu.VMEM((n, rows, depth), F32),
            pltpu.VMEM((n, rows, depth), BF16),
            dma((n,)), dma((n,)),
            dma((pairs, n)), dma((pairs, n)),
            dma((pairs, n)), dma((pairs, n)),
            dma((n,)), dma((n,)),
            dma((n,)), dma((n,)),
            dma((nreg,)), dma((nreg,)),
            dma((pairs, n)), dma((pairs, n)),
            dma((pairs, n)), dma((pairs, n)),
            dma((n,)), dma((n,)),
        ],
        compiler_params=pltpu.CompilerParams(
            collective_id=0, has_side_effects=True, vmem_limit_bytes=60 * 1024 * 1024),
        cost_estimate=pl.CostEstimate(
            flops=6 * n * nbr * rows * rows * depth, bytes_accessed=8 * rows * width,
            transcendentals=0),
    )(phi, hphi, extents, columns, kernel)


def solution(mesh):
    return jax.shard_map(
        shards,
        mesh=mesh,
        in_specs=(P("group", "region"), P("group", "region"), P("group", None), P(), P()),
        out_specs=(P("group", "region"), P("group", None, None, None)),
        check_vma=False,
    )
```

```python
import functools

import jax
import jax.numpy as jnp
from jax import lax
from jax.experimental import pallas as pl
from jax.experimental.pallas import tpu as pltpu
from jax.sharding import PartitionSpec as P

F32 = jnp.float32
BF16 = jnp.bfloat16


def body(n, nreg, phi, hphi, ext, colh, ker, grad, lag,
         col, colsem, ysend, rsend, src, gridp, gridh, shift, part, cbuf, ybuf, red, gbuf, low, fbuf, kh, ret,
         as_, ar, cs, cr, ys, yr, gs, gr, ls, lr, fs, fr, lys, lyr, lcs, lcr, bs, br):
    rows, width = phi.shape
    depth = width // n
    nbr = col.shape[0]
    pairs = nreg // 2
    slab = rows // nreg
    me = lax.axis_index("group")
    r = lax.axis_index("region")
    q = r // 2
    c = r % 2
    partner = 2 * q + 1 - c

    def to_group(a, b, s1, s2, k):
        return pltpu.make_async_remote_copy(
            src_ref=a, dst_ref=b, send_sem=s1, recv_sem=s2,
            device_id={"group": k}, device_id_type=pl.DeviceIdType.MESH)

    def to_region(a, b, s1, s2, k):
        return pltpu.make_async_remote_copy(
            src_ref=a, dst_ref=b, send_sem=s1, recv_sem=s2,
            device_id={"region": k}, device_id_type=pl.DeviceIdType.MESH)

    def each(lo, hi, f):
        def step(s, carry):
            f(s)
            return carry
        lax.fori_loop(lo, hi, step, 0)

    half = n // 2
    base = me // half * half
    place = me % half

    def up(s):
        start = jnp.where(s <= half, half - base, base)
        return start + lax.rem(place + jnp.where(s <= half, s - 1, s - half), half)

    def down(s):
        start = jnp.where(s <= half, half - base, base)
        return start + lax.rem(place + n - jnp.where(s <= half, s - 1, s - half), half)

    rup = lambda t: lax.rem(r + t, nreg)
    qup = lambda t: lax.rem(q + t, pairs)

    barrier = pltpu.get_barrier_semaphore()
    each(1, n, lambda s: pl.semaphore_signal(
        barrier, inc=1, device_id={"group": up(s)}, device_id_type=pl.DeviceIdType.MESH))
    each(1, nreg, lambda t: pl.semaphore_signal(
        barrier, inc=1, device_id={"region": rup(t)}, device_id_type=pl.DeviceIdType.MESH))

    fetch = pltpu.make_async_copy(colh, col, colsem)
    fetch.start()
    bounds = jnp.transpose(jnp.concatenate([ext[...]] * 4, axis=0))
    first = bounds[:, 0:1]
    last = bounds[:, 1:2]

    def inside(k):
        point = r * width + k * depth + lax.broadcasted_iota(jnp.int32, (rows, depth), 1)
        return (point >= first) & (point < last)

    def cut(k):
        return pl.ds(pl.multiple_of(k * depth, 128), depth)

    def masked(ref, k):
        return jnp.where(inside(k), ref[:, cut(k)].astype(F32), 0.0).astype(BF16)

    def shifted(k):
        shift[k] = (gridh[k].astype(F32) + 0.5 * gridp[k].astype(F32)).astype(BF16)

    gridp[me] = masked(phi, me)
    gridh[me] = masked(hphi, me)
    shifted(me)
    pl.semaphore_wait(barrier, n - 1 + nreg - 1)

    grids = (gridp, gridh)

    def out_copy(i, k):
        return to_group(src.at[k, i], grids[i].at[me], as_.at[k, i], ar.at[me, i], k)

    def in_wait(i, k):
        to_group(src.at[k, i], grids[i].at[k], as_.at[k, i], ar.at[k, i], k).wait_recv()

    def send_out(i, ref):
        def one(s):
            k = up(s)
            src[k, i] = masked(ref, k)
            out_copy(i, k).start()
        each(1, n, one)
    send_out(1, hphi)
    send_out(0, phi)
    fetch.wait()
    each(1, n, lambda s: in_wait(1, down(s)))

    def image(a):
        total = jnp.zeros((rows, depth), F32)
        for j in range(nbr):
            total = total + jnp.dot(ker[a, j], gridh[col[j, a]], preferred_element_type=F32)
        kh[a] = total
    each(0, n, image)

    def take_in(s):
        k = down(s)
        in_wait(0, k)
        shifted(k)
    each(1, n, take_in)

    def core_copy(p, a):
        return to_region(part.at[1 - c, p, a], cbuf.at[p, a], cs.at[p, a], cr.at[p, a], partner)

    def partial(s):
        a = up(s)
        left = gridp[a]
        for j in range(nbr):
            res = lax.dot_general(left, shift[col[j, a]], (((1,), (1,)), ((), ())),
                                  preferred_element_type=F32)
            for i in range(nreg):
                part[i % 2, i // 2, a, j] = res[i * slab:(i + 1) * slab]
        each(1, pairs + 1, lambda t: core_copy(qup(t), a).start())
    def y_copy(p, a):
        return to_region(ysend.at[p, a], ybuf.at[q, a], ys.at[p, a], yr.at[q, a], 2 * p + c)

    def y_wait(p, a):
        to_region(ysend.at[p, a], ybuf.at[p, a], ys.at[p, a], yr.at[p, a], 2 * p + c).wait_recv()

    def forward(s):
        a = up(s)

        def one(t):
            p = qup(t)
            core_copy(p, a).wait_recv()
            ysend[p, a] = (part[c, p, a] + cbuf[p, a]).astype(BF16)
            y_copy(p, a).start()
        each(1, pairs, one)

    partial(1)

    def both(s):
        partial(s)
        forward(s - 1)
    each(2, n + 1, both)
    forward(n)

    def red_copy(k):
        return to_group(rsend.at[k], gbuf.at[me], gs.at[k], gr.at[me], k)

    def reduce_one(a):
        core_copy(q, a).wait_recv()
        red[a] = part[c, q, a] + cbuf[q, a]

        def one(t):
            p = qup(t)
            y_wait(p, a)
            red[a] = red[a] + ybuf[p, a].astype(F32)
        each(1, pairs, one)

    def reduce_send(s):
        a = up(s)
        reduce_one(a)
        rsend[a] = red[a].astype(BF16)
        red_copy(a).start()
    each(1, n, reduce_send)
    reduce_one(me)

    def gather_sum(s):
        k = down(s)
        to_group(rsend.at[k], gbuf.at[k], gs.at[k], gr.at[k], k).wait_recv()
        red[me] = red[me] + gbuf[k].astype(F32)
    each(1, n, gather_sum)

    slot = lax.broadcasted_iota(jnp.int32, (nbr, slab, rows), 0)
    row = r * slab + lax.broadcasted_iota(jnp.int32, (nbr, slab, rows), 1)
    column = lax.broadcasted_iota(jnp.int32, (nbr, slab, rows), 2)
    eye = jnp.where((slot == 0) & (row == column), 0.5, 0.0)
    full = red[me] * (1.0 / width) - eye
    fbuf[r] = full
    low[c, q, me] = full.astype(BF16)

    def low_copy(k):
        return to_group(low.at[c, q, me], low.at[c, q, me], ls.at[k], lr.at[me], k)

    def low_wait(k):
        to_group(low.at[c, q, k], low.at[c, q, k], ls.at[k], lr.at[k], k).wait_recv()

    def ly_copy(p, k):
        return to_region(low.at[c, q, k], low.at[c, q, k], lys.at[p, k], lyr.at[q, k], 2 * p + c)

    def ly_wait(p, k):
        to_region(low.at[c, p, k], low.at[c, p, k], lys.at[p, k], lyr.at[p, k],
                  2 * p + c).wait_recv()

    def lc_copy(p, k):
        return to_region(low.at[c, p, k], low.at[c, p, k], lcs.at[p, k], lcr.at[p, k], partner)

    def lc_wait(p, k):
        to_region(low.at[1 - c, p, k], low.at[1 - c, p, k], lcs.at[p, k], lcr.at[p, k],
                  partner).wait_recv()

    def full_copy(i):
        return to_region(fbuf.at[r], fbuf.at[r], fs.at[i], fr.at[r], i)

    each(1, n, lambda s: low_copy(up(s)).start())
    each(1, pairs, lambda t: ly_copy(qup(t), me).start())
    lc_copy(q, me).start()

    def spread(s):
        k = down(s)
        low_wait(k)
        each(1, pairs, lambda t: ly_copy(qup(t), k).start())
        lc_copy(q, k).start()
    each(1, n, spread)
    each(1, nreg, lambda t: full_copy(rup(t)).start())

    def relay(s):
        k = down(s)

        def one(t):
            p = qup(t)
            ly_wait(p, k)
            lc_copy(p, k).start()
        each(1, pairs, one)
    relay(1)

    def back_copy(a):
        return to_group(shift.at[a], ret.at[me], bs.at[a], br.at[me], a)

    def descend(a):
        each(0, pairs, lambda p: lc_wait(p, a))
        total = kh[a]
        for j in range(nbr):
            block = jnp.concatenate([low[i % 2, i // 2, a, j] for i in range(nreg)], axis=0)
            total = total - jnp.dot(block, gridp[col[j, a]], preferred_element_type=F32)
        return total.astype(BF16)

    def send_back(s):
        relay(s + 1)
        a = down(s)
        shift[a] = descend(a)
        back_copy(a).start()
    each(1, n, send_back)

    def store(k, value):
        grad[:, cut(k)] = jnp.where(inside(k), value.astype(F32), 0.0).astype(BF16)

    store(me, descend(me))

    def finish(s):
        k = up(s)
        to_group(shift.at[k], ret.at[k], bs.at[k], br.at[k], k).wait_recv()
        store(k, ret[k])
    each(1, n, finish)

    def full_wait(t):
        i = rup(t)
        to_region(fbuf.at[i], fbuf.at[i], fs.at[i], fr.at[i], i).wait_recv()
    each(1, nreg, full_wait)
    for i in range(nreg):
        for j in range(nbr):
            lag[0, j, i * slab:(i + 1) * slab, :] = fbuf[i, j]

    def drain(s):
        k = up(s)
        out_copy(0, k).wait_send()
        out_copy(1, k).wait_send()
        red_copy(k).wait_send()
        low_copy(k).wait_send()
        back_copy(k).wait_send()
    each(1, n, drain)
    each(1, nreg, lambda t: full_copy(rup(t)).wait_send())

    def drain_region(a):
        def own(p):
            core_copy(p, a).wait_send()
            lc_copy(p, a).wait_send()

        def other(t):
            y_copy(qup(t), a).wait_send()
            ly_copy(qup(t), a).wait_send()
        each(0, pairs, own)
        each(1, pairs, other)
    each(0, n, drain_region)


def shards(phi, hphi, extents, columns, kernel):
    rows, width = phi.shape
    n = lax.axis_size("group")
    nreg = lax.axis_size("region")
    nbr = columns.shape[1]
    depth = width // n
    pairs = nreg // 2
    slab = rows // nreg
    dma = pltpu.SemaphoreType.DMA
    vmem = pl.BlockSpec(memory_space=pltpu.VMEM)
    return pl.pallas_call(
        functools.partial(body, n, nreg),
        out_shape=(jax.ShapeDtypeStruct((rows, width), BF16),
                   jax.ShapeDtypeStruct((1, nbr, rows, rows), F32)),
        in_specs=[vmem, vmem, vmem, pl.BlockSpec(memory_space=pl.ANY), vmem],
        out_specs=(vmem, vmem),
        scratch_shapes=[
            pltpu.SMEM(columns.shape[::-1], jnp.int32),
            dma(()),
            pltpu.VMEM((pairs, n, nbr, slab, rows), BF16),
            pltpu.VMEM((n, nbr, slab, rows), BF16),
            pltpu.VMEM((n, 2, rows, depth), BF16),
            pltpu.VMEM((n, rows, depth), BF16),
            pltpu.VMEM((n, rows, depth), BF16),
            pltpu.VMEM((n, rows, depth), BF16),
            pltpu.VMEM((2, pairs, n, nbr, slab, rows), F32),
            pltpu.VMEM((pairs, n, nbr, slab, rows), F32),
            pltpu.VMEM((pairs, n, nbr, slab, rows), BF16),
            pltpu.VMEM((n, nbr, slab, rows), F32),
            pltpu.VMEM((n, nbr, slab, rows), BF16),
            pltpu.VMEM((2, pairs, n, nbr, slab, rows), BF16),
            pltpu.VMEM((nreg, nbr, slab, rows), F32),
            pltpu.VMEM((n, rows, depth), F32),
            pltpu.VMEM((n, rows, depth), BF16),
            dma((n, 2)), dma((n, 2)),
            dma((pairs, n)), dma((pairs, n)),
            dma((pairs, n)), dma((pairs, n)),
            dma((n,)), dma((n,)),
            dma((n,)), dma((n,)),
            dma((nreg,)), dma((nreg,)),
            dma((pairs, n)), dma((pairs, n)),
            dma((pairs, n)), dma((pairs, n)),
            dma((n,)), dma((n,)),
        ],
        compiler_params=pltpu.CompilerParams(
            collective_id=0, has_side_effects=True, vmem_limit_bytes=60 * 1024 * 1024),
        cost_estimate=pl.CostEstimate(
            flops=6 * n * nbr * rows * rows * depth, bytes_accessed=8 * rows * width,
            transcendentals=0),
    )(phi, hphi, extents.T, columns.T, kernel)


def solution(mesh):
    return jax.shard_map(
        shards,
        mesh=mesh,
        in_specs=(P("group", "region"), P("group", "region"), P("group", None), P(), P()),
        out_specs=(P("group", "region"), P("group", None, None, None)),
        check_vma=False,
    )
```

```python
import functools

import jax
import jax.numpy as jnp
from jax import lax
from jax.experimental import pallas as pl
from jax.experimental.pallas import tpu as pltpu
from jax.sharding import PartitionSpec as P

F32 = jnp.float32
BF16 = jnp.bfloat16


def body(n, nreg, phi, hphi, ext, colh, ker, grad, lag,
         col, colsem, ysend, rsend, src, gridp, gridh, shift, part, cbuf, ybuf, red, gbuf, low, fbuf, kh, ret,
         as_, ar, cs, cr, ys, yr, gs, gr, ls, lr, fs, fr, lys, lyr, lcs, lcr, bs, br):
    rows, width = phi.shape
    depth = width // n
    nbr = col.shape[0]
    pairs = nreg // 2
    slab = rows // nreg
    me = lax.axis_index("group")
    r = lax.axis_index("region")
    q = r // 2
    c = r % 2
    partner = 2 * q + 1 - c

    def to_group(a, b, s1, s2, k):
        return pltpu.make_async_remote_copy(
            src_ref=a, dst_ref=b, send_sem=s1, recv_sem=s2,
            device_id={"group": k}, device_id_type=pl.DeviceIdType.MESH)

    def to_region(a, b, s1, s2, k):
        return pltpu.make_async_remote_copy(
            src_ref=a, dst_ref=b, send_sem=s1, recv_sem=s2,
            device_id={"region": k}, device_id_type=pl.DeviceIdType.MESH)

    def each(lo, hi, f):
        def step(s, carry):
            f(s)
            return carry
        lax.fori_loop(lo, hi, step, 0)

    half = n // 2

    def up(s):
        turn = s // 2 % half + s % 2 * half
        total, bit = 0, 1
        while bit < n:
            total = total + (me // bit + turn // bit) % 2 * bit
            bit = 2 * bit
        return total

    down = up

    rup = lambda t: lax.rem(r + t, nreg)
    qup = lambda t: lax.rem(q + t, pairs)

    barrier = pltpu.get_barrier_semaphore()
    each(1, n, lambda s: pl.semaphore_signal(
        barrier, inc=1, device_id={"group": up(s)}, device_id_type=pl.DeviceIdType.MESH))
    each(1, nreg, lambda t: pl.semaphore_signal(
        barrier, inc=1, device_id={"region": rup(t)}, device_id_type=pl.DeviceIdType.MESH))

    fetch = pltpu.make_async_copy(colh, col, colsem)
    fetch.start()
    bounds = jnp.transpose(jnp.concatenate([ext[...]] * 4, axis=0))
    first = bounds[:, 0:1]
    last = bounds[:, 1:2]

    def inside(k):
        point = r * width + k * depth + lax.broadcasted_iota(jnp.int32, (rows, depth), 1)
        return (point >= first) & (point < last)

    def cut(k):
        return pl.ds(pl.multiple_of(k * depth, 128), depth)

    def masked(ref, k):
        return jnp.where(inside(k), ref[:, cut(k)].astype(F32), 0.0).astype(BF16)

    def shifted(k):
        shift[k] = (gridh[k].astype(F32) + 0.5 * gridp[k].astype(F32)).astype(BF16)

    gridp[me] = masked(phi, me)
    gridh[me] = masked(hphi, me)
    shifted(me)
    pl.semaphore_wait(barrier, n - 1 + nreg - 1)

    grids = (gridp, gridh)

    def out_copy(i, k):
        return to_group(src.at[k, i], grids[i].at[me], as_.at[k, i], ar.at[me, i], k)

    def in_wait(i, k):
        to_group(src.at[k, i], grids[i].at[k], as_.at[k, i], ar.at[k, i], k).wait_recv()

    def send_out(i, ref):
        def one(s):
            k = up(s)
            src[k, i] = masked(ref, k)
            out_copy(i, k).start()
        each(1, n, one)
    send_out(1, hphi)
    send_out(0, phi)
    fetch.wait()
    each(1, n, lambda s: in_wait(1, down(s)))

    def image(a):
        total = jnp.zeros((rows, depth), F32)
        for j in range(nbr):
            total = total + jnp.dot(ker[a, j], gridh[col[j, a]], preferred_element_type=F32)
        kh[a] = total
    each(0, n, image)

    def take_in(s):
        k = down(s)
        in_wait(0, k)
        shifted(k)
    each(1, n, take_in)

    def core_copy(p, a):
        return to_region(part.at[1 - c, p, a], cbuf.at[p, a], cs.at[p, a], cr.at[p, a], partner)

    def partial(s):
        a = up(s)
        left = gridp[a]
        for j in range(nbr):
            res = lax.dot_general(left, shift[col[j, a]], (((1,), (1,)), ((), ())),
                                  preferred_element_type=F32)
            for i in range(nreg):
                part[i % 2, i // 2, a, j] = res[i * slab:(i + 1) * slab]
        each(1, pairs + 1, lambda t: core_copy(qup(t), a).start())
    def y_copy(p, a):
        return to_region(ysend.at[p, a], ybuf.at[q, a], ys.at[p, a], yr.at[q, a], 2 * p + c)

    def y_wait(p, a):
        to_region(ysend.at[p, a], ybuf.at[p, a], ys.at[p, a], yr.at[p, a], 2 * p + c).wait_recv()

    def forward(s):
        a = up(s)

        def one(t):
            p = qup(t)
            core_copy(p, a).wait_recv()
            ysend[p, a] = (part[c, p, a] + cbuf[p, a]).astype(BF16)
            y_copy(p, a).start()
        each(1, pairs, one)

    partial(1)

    def both(s):
        partial(s)
        forward(s - 1)
    each(2, n + 1, both)
    forward(n)

    def red_copy(k):
        return to_group(rsend.at[k], gbuf.at[me], gs.at[k], gr.at[me], k)

    def reduce_one(a):
        core_copy(q, a).wait_recv()
        red[a] = part[c, q, a] + cbuf[q, a]

        def one(t):
            p = qup(t)
            y_wait(p, a)
            red[a] = red[a] + ybuf[p, a].astype(F32)
        each(1, pairs, one)

    def reduce_send(s):
        a = up(s)
        reduce_one(a)
        rsend[a] = red[a].astype(BF16)
        red_copy(a).start()
    each(1, n, reduce_send)
    reduce_one(me)

    def gather_sum(s):
        k = down(s)
        to_group(rsend.at[k], gbuf.at[k], gs.at[k], gr.at[k], k).wait_recv()
        red[me] = red[me] + gbuf[k].astype(F32)
    each(1, n, gather_sum)

    slot = lax.broadcasted_iota(jnp.int32, (nbr, slab, rows), 0)
    row = r * slab + lax.broadcasted_iota(jnp.int32, (nbr, slab, rows), 1)
    column = lax.broadcasted_iota(jnp.int32, (nbr, slab, rows), 2)
    eye = jnp.where((slot == 0) & (row == column), 0.5, 0.0)
    full = red[me] * (1.0 / width) - eye
    fbuf[r] = full
    low[c, q, me] = full.astype(BF16)

    def low_copy(k):
        return to_group(low.at[c, q, me], low.at[c, q, me], ls.at[k], lr.at[me], k)

    def low_wait(k):
        to_group(low.at[c, q, k], low.at[c, q, k], ls.at[k], lr.at[k], k).wait_recv()

    def ly_copy(p, k):
        return to_region(low.at[c, q, k], low.at[c, q, k], lys.at[p, k], lyr.at[q, k], 2 * p + c)

    def ly_wait(p, k):
        to_region(low.at[c, p, k], low.at[c, p, k], lys.at[p, k], lyr.at[p, k],
                  2 * p + c).wait_recv()

    def lc_copy(p, k):
        return to_region(low.at[c, p, k], low.at[c, p, k], lcs.at[p, k], lcr.at[p, k], partner)

    def lc_wait(p, k):
        to_region(low.at[1 - c, p, k], low.at[1 - c, p, k], lcs.at[p, k], lcr.at[p, k],
                  partner).wait_recv()

    def full_copy(i):
        return to_region(fbuf.at[r], fbuf.at[r], fs.at[i], fr.at[r], i)

    each(1, n, lambda s: low_copy(up(s)).start())
    each(1, pairs, lambda t: ly_copy(qup(t), me).start())
    lc_copy(q, me).start()

    def spread(s):
        k = down(s)
        low_wait(k)
        each(1, pairs, lambda t: ly_copy(qup(t), k).start())
        lc_copy(q, k).start()
    each(1, n, spread)
    each(1, nreg, lambda t: full_copy(rup(t)).start())

    def relay(s):
        k = down(s)

        def one(t):
            p = qup(t)
            ly_wait(p, k)
            lc_copy(p, k).start()
        each(1, pairs, one)
    relay(1)

    def back_copy(a):
        return to_group(shift.at[a], ret.at[me], bs.at[a], br.at[me], a)

    def descend(a):
        each(0, pairs, lambda p: lc_wait(p, a))
        total = kh[a]
        for j in range(nbr):
            block = jnp.concatenate([low[i % 2, i // 2, a, j] for i in range(nreg)], axis=0)
            total = total - jnp.dot(block, gridp[col[j, a]], preferred_element_type=F32)
        return total.astype(BF16)

    def send_back(s):
        relay(s + 1)
        a = down(s)
        shift[a] = descend(a)
        back_copy(a).start()
    each(1, n, send_back)

    def store(k, value):
        grad[:, cut(k)] = jnp.where(inside(k), value.astype(F32), 0.0).astype(BF16)

    store(me, descend(me))

    def finish(s):
        k = up(s)
        to_group(shift.at[k], ret.at[k], bs.at[k], br.at[k], k).wait_recv()
        store(k, ret[k])
    each(1, n, finish)

    def full_wait(t):
        i = rup(t)
        to_region(fbuf.at[i], fbuf.at[i], fs.at[i], fr.at[i], i).wait_recv()
    each(1, nreg, full_wait)
    for i in range(nreg):
        for j in range(nbr):
            lag[0, j, i * slab:(i + 1) * slab, :] = fbuf[i, j]

    def drain(s):
        k = up(s)
        out_copy(0, k).wait_send()
        out_copy(1, k).wait_send()
        red_copy(k).wait_send()
        low_copy(k).wait_send()
        back_copy(k).wait_send()
    each(1, n, drain)
    each(1, nreg, lambda t: full_copy(rup(t)).wait_send())

    def drain_region(a):
        def own(p):
            core_copy(p, a).wait_send()
            lc_copy(p, a).wait_send()

        def other(t):
            y_copy(qup(t), a).wait_send()
            ly_copy(qup(t), a).wait_send()
        each(0, pairs, own)
        each(1, pairs, other)
    each(0, n, drain_region)


def shards(phi, hphi, extents, columns, kernel):
    rows, width = phi.shape
    n = lax.axis_size("group")
    nreg = lax.axis_size("region")
    nbr = columns.shape[1]
    depth = width // n
    pairs = nreg // 2
    slab = rows // nreg
    dma = pltpu.SemaphoreType.DMA
    vmem = pl.BlockSpec(memory_space=pltpu.VMEM)
    return pl.pallas_call(
        functools.partial(body, n, nreg),
        out_shape=(jax.ShapeDtypeStruct((rows, width), BF16),
                   jax.ShapeDtypeStruct((1, nbr, rows, rows), F32)),
        in_specs=[vmem, vmem, vmem, pl.BlockSpec(memory_space=pl.ANY), vmem],
        out_specs=(vmem, vmem),
        scratch_shapes=[
            pltpu.SMEM(columns.shape[::-1], jnp.int32),
            dma(()),
            pltpu.VMEM((pairs, n, nbr, slab, rows), BF16),
            pltpu.VMEM((n, nbr, slab, rows), BF16),
            pltpu.VMEM((n, 2, rows, depth), BF16),
            pltpu.VMEM((n, rows, depth), BF16),
            pltpu.VMEM((n, rows, depth), BF16),
            pltpu.VMEM((n, rows, depth), BF16),
            pltpu.VMEM((2, pairs, n, nbr, slab, rows), F32),
            pltpu.VMEM((pairs, n, nbr, slab, rows), F32),
            pltpu.VMEM((pairs, n, nbr, slab, rows), BF16),
            pltpu.VMEM((n, nbr, slab, rows), F32),
            pltpu.VMEM((n, nbr, slab, rows), BF16),
            pltpu.VMEM((2, pairs, n, nbr, slab, rows), BF16),
            pltpu.VMEM((nreg, nbr, slab, rows), F32),
            pltpu.VMEM((n, rows, depth), F32),
            pltpu.VMEM((n, rows, depth), BF16),
            dma((n, 2)), dma((n, 2)),
            dma((pairs, n)), dma((pairs, n)),
            dma((pairs, n)), dma((pairs, n)),
            dma((n,)), dma((n,)),
            dma((n,)), dma((n,)),
            dma((nreg,)), dma((nreg,)),
            dma((pairs, n)), dma((pairs, n)),
            dma((pairs, n)), dma((pairs, n)),
            dma((n,)), dma((n,)),
        ],
        compiler_params=pltpu.CompilerParams(
            collective_id=0, has_side_effects=True, vmem_limit_bytes=60 * 1024 * 1024),
        cost_estimate=pl.CostEstimate(
            flops=6 * n * nbr * rows * rows * depth, bytes_accessed=8 * rows * width,
            transcendentals=0),
    )(phi, hphi, extents.T, columns.T, kernel)


def solution(mesh):
    return jax.shard_map(
        shards,
        mesh=mesh,
        in_specs=(P("group", "region"), P("group", "region"), P("group", None), P(), P()),
        out_specs=(P("group", "region"), P("group", None, None, None)),
        check_vma=False,
    )
```
